32 devices in a mesh: groups: 2 (over x), wide: 8 (over z, y), narrow: 2 (over core).
Axes of the slice: x: 2, y: 2, z: 4, core: 2. Of those that a mesh axis runs over, the one named last changes fastest.
Arguments:
- gate_pre: bfloat16 [512, 26624], P(('groups', 'narrow'), 'wide'), parts along dimension 0, may hold values from -6 to 6
- up_pre: bfloat16 [512, 26624], P(('groups', 'narrow'), 'wide'), parts along dimension 0, may hold values from -6 to 6
- down_weight: bfloat16 [26624, 8192], P('wide', 'narrow'), may hold values from -0.0390625 to 0.0390625
Outputs:
- mixed: bfloat16 [512, 8192], P(('groups', 'wide'), 'narrow'), parts along dimension 0
The draws below stay inside these ranges and needn't reach their ends.
There are 2 independent parts, one for each index of `groups`. The reference program is written for one: setup_inputs(seed, part) draws one part's arguments, and reference() takes and returns one part's arrays. A program takes and returns all parts, laid end to end along the dimension named above; an argument that names none is the same for every part. Nothing has to cross between parts.
All inputs are finite; a program needn't handle non-finite values.
Results may differ from the reference program's by a relative error of at most 0.0049.
Values may be sent and summed in bfloat16 or wider, within the bound.
A program may use at most 128 MiB of HBM per device.

```python
import jax
import jax.numpy as jnp

D = 8192
FF = 26624
TOKENS = 256


def raised(result, key, source, target, parts, factor):
    owner, partner = [(jnp.arange(result.shape[axis_at]) // (result.shape[axis_at] // parts)).reshape([-1 if axis == axis_at else 1 for axis in range(result.ndim)]) for axis_at in (source, target)]
    chosen = jax.random.permutation(key, parts)[partner]
    strong = (owner == chosen) | (owner == (partner + parts // 2) % parts)
    return jnp.where(strong, factor * result, result)


def levels(rng, extent, pieces, smallest, high):
    def one(axis_at, parts):
        steps = jax.random.uniform(jax.random.fold_in(jax.random.fold_in(rng, 6), axis_at), (parts,), jnp.float32, smallest / len(pieces), high / len(pieces))
        return jnp.repeat(jnp.exp(steps), extent[axis_at] // parts).reshape((-1,) + (1,) * (len(extent) - axis_at - 1))

    level = one(*pieces[0])
    for cut in pieces[1:]:
        level = level * one(*cut)
    return level


def gaussian(own_key, dims, deviation, most, shards=(), held_as=jnp.bfloat16):
    values = jax.random.normal(own_key, dims, jnp.float32) * deviation
    if len(shards) > 0:
        values = levels(own_key, dims, shards, -0.22, 0.18) * values
    return jnp.clip(values, min=-most, max=most).astype(held_as)


def heavy_noise(stream_key, extent, spread, reach, pieces, heavy, dtype=jnp.bfloat16):
    entries = spread * jax.random.normal(stream_key, extent, jnp.float32)
    if pieces:
        entries = entries * levels(stream_key, extent, pieces, -0.22, 0.18)
    return jnp.clip(raised(entries, jax.random.fold_in(stream_key, 3), *heavy), -reach, reach).astype(dtype)


def setup_inputs(seed: int = 0, part: int = 0) -> dict:
    seeds = jax.random.split(jax.random.key(seed), 4)
    part_splits = jax.random.split(jax.random.fold_in(seeds[3], part), 4)
    gate_pre = gaussian(part_splits[0], (TOKENS, FF), 1.0, 6.0, ((0, 2), (1, 8)))
    up_pre = heavy_noise(part_splits[1], (TOKENS, FF), 1.0, 6.0, ((0, 2), (1, 8)), (1, 0, 8, 2.0))
    down_weight = gaussian(seeds[2], (FF, D), FF ** -0.5, 0.0390625, ((0, 8), (1, 2)))
    return dict(gate_pre=gate_pre, up_pre=up_pre, down_weight=down_weight)


def reference(gate_pre, up_pre, down_weight):
    hidden = (jax.nn.silu(gate_pre.astype(jnp.float32)) * up_pre.astype(jnp.float32)).astype(jnp.bfloat16)
    return jnp.dot(hidden, down_weight, preferred_element_type=jnp.float32).astype(jnp.bfloat16)
```

```python
import functools

import jax
import jax.numpy as jnp
from jax import lax
from jax.experimental import pallas as pl
from jax.experimental.pallas import tpu as pltpu
from jax.sharding import PartitionSpec as P

MESH = pl.DeviceIdType.MESH
TILE = 512


def reverse(value, bits):
    return sum(((value >> i) & 1) << (bits - 1 - i) for i in range(bits))


def kernel(stages, block, gate_hbm, up_hbm, weight_hbm, out_ref, gate, up, hidden, weight, acc, *rest):
    sends, recvs = rest[:stages], rest[stages : 2 * stages]
    in_sem, weight_sem, gather_send, gather_recv, send_sem, recv_sem = rest[2 * stages :]
    chunks, depth, tile = weight.shape
    mine = hidden.shape[0]
    tokens = 2 * mine * block
    wide, core = lax.axis_index("wide"), lax.axis_index("narrow")
    bits = [(wide // 2**k) % 2 for k in range(stages)]
    partner = [wide + (1 - 2 * bits[k]) * 2**k for k in range(stages)]

    def fetch(j):
        rows = pl.ds(j * block, block)
        return (
            pltpu.make_async_copy(gate_hbm.at[rows], gate.at[rows], in_sem.at[0, j]),
            pltpu.make_async_copy(up_hbm.at[rows], up.at[rows], in_sem.at[1, j]),
        )

    def weight_copy(c):
        return pltpu.make_async_copy(
            weight_hbm.at[:, pl.ds(pl.multiple_of(c * tile, tile), tile)], weight.at[c], weight_sem.at[c]
        )

    def gather(j):
        place = hidden.at[reverse(j, stages - 1), core]
        return pltpu.make_async_remote_copy(
            src_ref=place,
            dst_ref=place,
            send_sem=gather_send.at[j],
            recv_sem=gather_recv.at[j],
            device_id={"narrow": 1 - core},
            device_id_type=MESH,
        )

    def exchange(k, c):
        return pltpu.make_async_remote_copy(
            src_ref=sends[k].at[c],
            dst_ref=recvs[k].at[c],
            send_sem=send_sem.at[k, c],
            recv_sem=recv_sem.at[k, c],
            device_id={"wide": partner[k]},
            device_id_type=MESH,
        )

    for j in range(mine):
        for copy in fetch(j):
            copy.start()
    for c in range(chunks):
        weight_copy(c).start()

    barrier = pltpu.get_barrier_semaphore()
    pl.semaphore_signal(barrier, inc=1, device_id={"narrow": 1 - core}, device_id_type=MESH)
    for k in range(stages):
        pl.semaphore_signal(barrier, inc=1, device_id={"wide": partner[k]}, device_id_type=MESH)
    pl.semaphore_wait(barrier, stages + 1)

    for j in range(mine):
        for copy in fetch(j):
            copy.wait()
        rows = pl.ds(j * block, block)
        value = jax.nn.silu(gate[rows].astype(jnp.float32)) * up[rows].astype(jnp.float32)
        hidden[reverse(j, stages - 1), core] = value.astype(jnp.bfloat16)
        gather(j).start()
    for j in range(mine):
        gather(j).wait()

    start = [0]
    for k in range(stages):
        start.append(start[k] + bits[k] * (tokens >> (k + 1)))

    def multiply(c):
        weight_copy(c).wait()
        acc[c] = jnp.dot(
            hidden[...].reshape(tokens, depth), weight[c], preferred_element_type=jnp.float32
        )
        half = tokens // 2
        sends[0][c] = acc[c, pl.ds(pl.multiple_of((1 - bits[0]) * half, half), half)].astype(jnp.bfloat16)
        exchange(0, c).start()

    def reduce(k, c):
        exchange(k - 1, c).wait_recv()
        half = tokens >> (k + 1)
        other, own = (pl.multiple_of(bit * half, half) for bit in (1 - bits[k], bits[k]))
        base = pl.multiple_of(start[k], half)
        sends[k][c] = (
            acc[c, pl.ds(pl.multiple_of(base + other, half), half)]
            + recvs[k - 1][c, pl.ds(other, half)].astype(jnp.float32)
        ).astype(jnp.bfloat16)
        exchange(k, c).start()
        acc[c, pl.ds(pl.multiple_of(base + own, half), half)] += recvs[k - 1][c, pl.ds(own, half)].astype(
            jnp.float32
        )

    def finish(c):
        exchange(stages - 1, c).wait_recv()
        total = acc[c, pl.ds(pl.multiple_of(start[stages], block), block)] + recvs[stages - 1][c].astype(jnp.float32)
        out_ref[:, pl.ds(pl.multiple_of(c * tile, tile), tile)] = total.astype(jnp.bfloat16)

    @pl.loop(0, chunks + stages)
    def _(i):
        @pl.when(i < chunks // 2)
        def _():
            @pl.loop(0, 2)
            def _(half):
                multiply(2 * i + half)

        for k in range(1, stages):

            @pl.when((i >= k) & (i < chunks + k))
            def _():
                reduce(k, i - k)

        @pl.when(i >= stages)
        def _():
            finish(i - stages)

    @pl.loop(0, chunks)
    def _(c):
        for k in range(stages):
            exchange(k, c).wait_send()


def solution(mesh):
    wide = mesh.shape["wide"]
    stages = wide.bit_length() - 1

    def body(gate_pre, up_pre, down_weight):
        rows, depth = gate_pre.shape
        columns = down_weight.shape[1]
        mine = wide // 2
        block, tokens, chunks = rows // mine, 2 * rows, columns // TILE
        parts = [pltpu.VMEM((chunks, tokens >> (k + 1), TILE), jnp.bfloat16) for k in range(stages)]
        return pl.pallas_call(
            functools.partial(kernel, stages, block),
            out_shape=jax.ShapeDtypeStruct((block, columns), jnp.bfloat16),
            in_specs=[pl.BlockSpec(memory_space=pl.ANY)] * 3,
            out_specs=pl.BlockSpec(memory_space=pltpu.VMEM),
            scratch_shapes=[
                pltpu.VMEM((rows, depth), jnp.bfloat16),
                pltpu.VMEM((rows, depth), jnp.bfloat16),
                pltpu.VMEM((mine, 2, block, depth), jnp.bfloat16),
                pltpu.VMEM((chunks, depth, TILE), jnp.bfloat16),
                pltpu.VMEM((chunks, tokens, TILE), jnp.float32),
                *parts,
                *parts,
                pltpu.SemaphoreType.DMA((2, mine)),
                pltpu.SemaphoreType.DMA((chunks,)),
                pltpu.SemaphoreType.DMA((mine,)),
                pltpu.SemaphoreType.DMA((mine,)),
                pltpu.SemaphoreType.DMA((stages, chunks)),
                pltpu.SemaphoreType.DMA((stages, chunks)),
            ],
            cost_estimate=pl.CostEstimate(
                flops=2 * tokens * depth * columns, bytes_accessed=2 * depth * columns, transcendentals=rows * depth
            ),
            compiler_params=pltpu.CompilerParams(
                collective_id=0, has_side_effects=True, vmem_limit_bytes=60 * 2**20
            ),
        )(gate_pre, up_pre, down_weight)

    return jax.shard_map(
        body,
        mesh=mesh,
        in_specs=(
            P(("groups", "narrow"), "wide"),
            P(("groups", "narrow"), "wide"),
            P("wide", "narrow"),
        ),
        out_specs=P(("groups", "wide"), "narrow"),
        check_vma=False,
    )
```

```python
import functools

import jax
import jax.numpy as jnp
from jax import lax
from jax.experimental import pallas as pl
from jax.experimental.pallas import tpu as pltpu
from jax.sharding import PartitionSpec as P

MESH = pl.DeviceIdType.MESH
TILE = 512
CROSSED = 2


def reverse(value, bits):
    return sum(((value >> i) & 1) << (bits - 1 - i) for i in range(bits))


def kernel(stages, block, gate_hbm, up_hbm, weight_hbm, out_ref, gate, up, hidden, weight, acc, *rest):
    sends, recvs = rest[:stages], rest[stages : 2 * stages]
    in_sem, weight_sem, gather_send, gather_recv, send_sem, recv_sem = rest[2 * stages :]
    chunks, depth, tile = weight.shape
    mine = hidden.shape[0]
    tokens = 2 * mine * block
    wide, core = lax.axis_index("wide"), lax.axis_index("narrow")
    bits = [(wide // 2**k) % 2 for k in range(stages)]
    partner = [wide + (1 - 2 * bits[k]) * 2**k for k in range(stages)]

    def fetch(j):
        rows = pl.ds(j * block, block)
        return (
            pltpu.make_async_copy(gate_hbm.at[rows], gate.at[rows], in_sem.at[0, j]),
            pltpu.make_async_copy(up_hbm.at[rows], up.at[rows], in_sem.at[1, j]),
        )

    def weight_copy(c):
        return pltpu.make_async_copy(
            weight_hbm.at[:, pl.ds(pl.multiple_of(c * tile, tile), tile)], weight.at[c], weight_sem.at[c]
        )

    def gather(j):
        place = hidden.at[reverse(j, stages - 1), core]
        return pltpu.make_async_remote_copy(
            src_ref=place,
            dst_ref=place,
            send_sem=gather_send.at[j],
            recv_sem=gather_recv.at[j],
            device_id={"narrow": 1 - core},
            device_id_type=MESH,
        )

    def exchange(k, c, crossed=False):
        to = partner[1 - k] if crossed and k < 2 else partner[k]
        return pltpu.make_async_remote_copy(
            src_ref=sends[k].at[c],
            dst_ref=recvs[k].at[c],
            send_sem=send_sem.at[k, c],
            recv_sem=recv_sem.at[k, c],
            device_id={"wide": to},
            device_id_type=MESH,
        )

    first_crossed = chunks - CROSSED - 1
    straight = chunks - CROSSED

    def nth_straight(i):
        return i + (i // first_crossed) * CROSSED

    for j in range(mine):
        for copy in fetch(j):
            copy.start()
    for c in (0, *range(first_crossed, chunks - 1)):
        weight_copy(c).start()

    barrier = pltpu.get_barrier_semaphore()
    pl.semaphore_signal(barrier, inc=1, device_id={"narrow": 1 - core}, device_id_type=MESH)
    for k in range(stages):
        pl.semaphore_signal(barrier, inc=1, device_id={"wide": partner[k]}, device_id_type=MESH)
    pl.semaphore_wait(barrier, stages + 1)

    for j in range(mine):
        for copy in fetch(j):
            copy.wait()
        rows = pl.ds(j * block, block)
        value = jax.nn.silu(gate[rows].astype(jnp.float32)) * up[rows].astype(jnp.float32)
        hidden[reverse(j, stages - 1), core] = value.astype(jnp.bfloat16)
        gather(j).start()
    for i in range(1, 3):
        weight_copy(nth_straight(i)).start()
    for j in range(mine):
        gather(j).wait()

    b0, b1 = bits[:2]
    quarter = tokens // 4
    start = [None, None, 0]
    for k in range(2, stages):
        start.append(start[k] + bits[k] * (tokens >> (k + 1)))

    def multiply(c, crossed):
        weight_copy(c).wait()
        product = jnp.dot(hidden[...].reshape(tokens, depth), weight[c], preferred_element_type=jnp.float32)
        acc[c] = product.reshape(2, 2, quarter, tile)
        leaving = acc[c, :, 1 - b1] if crossed else acc[c, 1 - b0]
        sends[0][c] = leaving.astype(jnp.bfloat16)
        exchange(0, c, crossed).start()

    def second(c, crossed):
        exchange(0, c, crossed).wait_recv()
        o0, o1, other, own = (1 - b0, b1, 1 - b0, b0) if crossed else (b0, 1 - b1, 1 - b1, b1)
        sends[1][c] = (acc[c, o0, o1] + recvs[0][c, other].astype(jnp.float32)).astype(jnp.bfloat16)
        exchange(1, c, crossed).start()
        acc[c, b0, b1] += recvs[0][c, own].astype(jnp.float32)

    def later(k, c):
        exchange(k - 1, c).wait_recv()
        half = tokens >> (k + 1)
        other, own = (pl.multiple_of(bit * half, half) for bit in (1 - bits[k], bits[k]))
        sends[k][c] = (
            acc[c, b0, b1, pl.ds(pl.multiple_of(start[k] + other, half), half)]
            + recvs[k - 1][c, pl.ds(other, half)].astype(jnp.float32)
        ).astype(jnp.bfloat16)
        exchange(k, c).start()
        acc[c, b0, b1, pl.ds(pl.multiple_of(start[k] + own, half), half)] += recvs[k - 1][
            c, pl.ds(own, half)
        ].astype(jnp.float32)

    def finish(c):
        exchange(stages - 1, c).wait_recv()
        total = acc[c, b0, b1, pl.ds(pl.multiple_of(start[stages], block), block)]
        total += recvs[stages - 1][c].astype(jnp.float32)
        out_ref[:, pl.ds(pl.multiple_of(c * tile, tile), tile)] = total.astype(jnp.bfloat16)

    multiply(0, False)

    @pl.loop(first_crossed, chunks - 1)
    def _(c):
        multiply(c, True)

    @pl.loop(1, chunks + 2 * stages - 1)
    def _(i):
        @pl.when(i + 2 < straight)
        def _():
            weight_copy(nth_straight(i + 2)).start()

        @pl.when(i < straight)
        def _():
            multiply(nth_straight(i), False)

        @pl.when((i - 1 >= first_crossed) & (i - 1 < chunks - 1))
        def _():
            second(i - 1, True)

        @pl.when((i - 1 < first_crossed) | (i - 1 == chunks - 1))
        def _():
            second(i - 1, False)

        for k in range(2, stages):
            lag = 2 * k - 1

            @pl.when((i >= lag) & (i < chunks + lag))
            def _():
                later(k, i - lag)

        @pl.when(i >= 2 * stages - 1)
        def _():
            finish(i - (2 * stages - 1))

    @pl.loop(0, chunks)
    def _(c):
        for k in range(stages):
            exchange(k, c).wait_send()


def solution(mesh):
    wide = mesh.shape["wide"]
    stages = wide.bit_length() - 1

    def body(gate_pre, up_pre, down_weight):
        rows, depth = gate_pre.shape
        columns = down_weight.shape[1]
        mine = wide // 2
        block, tokens, chunks = rows // mine, 2 * rows, columns // TILE
        held = [(2, tokens // 4), *((tokens >> (k + 1),) for k in range(1, stages))]
        parts = [pltpu.VMEM((chunks, *rows_held, TILE), jnp.bfloat16) for rows_held in held]
        return pl.pallas_call(
            functools.partial(kernel, stages, block),
            out_shape=jax.ShapeDtypeStruct((block, columns), jnp.bfloat16),
            in_specs=[pl.BlockSpec(memory_space=pl.ANY)] * 3,
            out_specs=pl.BlockSpec(memory_space=pltpu.VMEM),
            scratch_shapes=[
                pltpu.VMEM((rows, depth), jnp.bfloat16),
                pltpu.VMEM((rows, depth), jnp.bfloat16),
                pltpu.VMEM((mine, 2, block, depth), jnp.bfloat16),
                pltpu.VMEM((chunks, depth, TILE), jnp.bfloat16),
                pltpu.VMEM((chunks, 2, 2, tokens // 4, TILE), jnp.float32),
                *parts,
                *parts,
                pltpu.SemaphoreType.DMA((2, mine)),
                pltpu.SemaphoreType.DMA((chunks,)),
                pltpu.SemaphoreType.DMA((mine,)),
                pltpu.SemaphoreType.DMA((mine,)),
                pltpu.SemaphoreType.DMA((stages, chunks)),
                pltpu.SemaphoreType.DMA((stages, chunks)),
            ],
            cost_estimate=pl.CostEstimate(
                flops=2 * tokens * depth * columns, bytes_accessed=2 * depth * columns, transcendentals=rows * depth
            ),
            compiler_params=pltpu.CompilerParams(
                collective_id=0, has_side_effects=True, vmem_limit_bytes=60 * 2**20
            ),
        )(gate_pre, up_pre, down_weight)

    return jax.shard_map(
        body,
        mesh=mesh,
        in_specs=(
            P(("groups", "narrow"), "wide"),
            P(("groups", "narrow"), "wide"),
            P("wide", "narrow"),
        ),
        out_specs=P(("groups", "wide"), "narrow"),
        check_vma=False,
    )
```

```python
import functools

import jax
import jax.numpy as jnp
from jax import lax
from jax.experimental import pallas as pl
from jax.experimental.pallas import tpu as pltpu
from jax.sharding import PartitionSpec as P

MESH = pl.DeviceIdType.MESH
TILE = 512
CROSSED = 2


def reverse(value, bits):
    return sum(((value >> i) & 1) << (bits - 1 - i) for i in range(bits))


def kernel(stages, block, gate_hbm, up_hbm, weight_hbm, out_ref, gate, up, hidden, weight, acc, *rest):
    sends, recvs = rest[:stages], rest[stages : 2 * stages]
    in_sem, weight_sem, gather_send, gather_recv, send_sem, recv_sem = rest[2 * stages :]
    chunks, depth, tile = weight.shape
    mine = hidden.shape[0]
    tokens = 2 * mine * block
    wide, core = lax.axis_index("wide"), lax.axis_index("narrow")
    bits = [(wide // 2**k) % 2 for k in range(stages)]
    partner = [wide + (1 - 2 * bits[k]) * 2**k for k in range(stages)]

    def fetch(j):
        rows = pl.ds(j * block, block)
        return (
            pltpu.make_async_copy(gate_hbm.at[rows], gate.at[rows], in_sem.at[0, j]),
            pltpu.make_async_copy(up_hbm.at[rows], up.at[rows], in_sem.at[1, j]),
        )

    def weight_copy(c):
        return pltpu.make_async_copy(
            weight_hbm.at[:, pl.ds(pl.multiple_of(c * tile, tile), tile)], weight.at[c], weight_sem.at[c]
        )

    def gather(j):
        place = hidden.at[reverse(j, stages - 1), core]
        return pltpu.make_async_remote_copy(
            src_ref=place,
            dst_ref=place,
            send_sem=gather_send.at[j],
            recv_sem=gather_recv.at[j],
            device_id={"narrow": 1 - core},
            device_id_type=MESH,
        )

    def exchange(k, c, crossed=False):
        to = partner[1 - k] if crossed and k < 2 else partner[k]
        return pltpu.make_async_remote_copy(
            src_ref=sends[k].at[c],
            dst_ref=recvs[k].at[c],
            send_sem=send_sem.at[k, c],
            recv_sem=recv_sem.at[k, c],
            device_id={"wide": to},
            device_id_type=MESH,
        )

    first_crossed = chunks - CROSSED - 1
    straight = chunks - CROSSED

    def nth_straight(i):
        return i + (i // first_crossed) * CROSSED

    for j in range(mine):
        for copy in fetch(j):
            copy.start()
    for c in (0, 1, *range(first_crossed, chunks - 1)):
        weight_copy(c).start()

    barrier = pltpu.get_barrier_semaphore()
    pl.semaphore_signal(barrier, inc=1, device_id={"narrow": 1 - core}, device_id_type=MESH)
    for k in range(stages):
        pl.semaphore_signal(barrier, inc=1, device_id={"wide": partner[k]}, device_id_type=MESH)
    pl.semaphore_wait(barrier, stages + 1)

    for j in range(mine):
        for copy in fetch(j):
            copy.wait()
        rows = pl.ds(j * block, block)
        value = jax.nn.silu(gate[rows].astype(jnp.float32)) * up[rows].astype(jnp.float32)
        hidden[reverse(j, stages - 1), core] = value.astype(jnp.bfloat16)
        gather(j).start()
    for i in range(2, 4):
        weight_copy(nth_straight(i)).start()
    for j in range(mine):
        gather(j).wait()

    b0, b1 = bits[:2]
    quarter = tokens // 4
    start = [None, None, 0]
    for k in range(2, stages):
        start.append(start[k] + bits[k] * (tokens >> (k + 1)))

    def multiply(c, crossed):
        weight_copy(c).wait()
        product = jnp.dot(hidden[...].reshape(tokens, depth), weight[c], preferred_element_type=jnp.float32)
        acc[c] = product.reshape(2, 2, quarter, tile)
        leaving = acc[c, :, 1 - b1] if crossed else acc[c, 1 - b0]
        sends[0][c] = leaving.astype(jnp.bfloat16)
        exchange(0, c, crossed).start()

    def second(c, crossed):
        exchange(0, c, crossed).wait_recv()
        o0, o1, other, own = (1 - b0, b1, 1 - b0, b0) if crossed else (b0, 1 - b1, 1 - b1, b1)
        sends[1][c] = (acc[c, o0, o1] + recvs[0][c, other].astype(jnp.float32)).astype(jnp.bfloat16)
        exchange(1, c, crossed).start()
        acc[c, b0, b1] += recvs[0][c, own].astype(jnp.float32)

    def later(k, c):
        exchange(k - 1, c).wait_recv()
        half = tokens >> (k + 1)
        other, own = (pl.multiple_of(bit * half, half) for bit in (1 - bits[k], bits[k]))
        sends[k][c] = (
            acc[c, b0, b1, pl.ds(pl.multiple_of(start[k] + other, half), half)]
            + recvs[k - 1][c, pl.ds(other, half)].astype(jnp.float32)
        ).astype(jnp.bfloat16)
        exchange(k, c).start()
        acc[c, b0, b1, pl.ds(pl.multiple_of(start[k] + own, half), half)] += recvs[k - 1][
            c, pl.ds(own, half)
        ].astype(jnp.float32)

    def finish(c):
        exchange(stages - 1, c).wait_recv()
        total = acc[c, b0, b1, pl.ds(pl.multiple_of(start[stages], block), block)]
        total += recvs[stages - 1][c].astype(jnp.float32)
        out_ref[:, pl.ds(pl.multiple_of(c * tile, tile), tile)] = total.astype(jnp.bfloat16)

    @pl.loop(0, 2)
    def _(c):
        multiply(c, False)

    @pl.loop(first_crossed, chunks - 1)
    def _(c):
        multiply(c, True)

    @pl.loop(1, chunks + 2 * stages - 1)
    def _(i):
        @pl.when(i + 3 < straight)
        def _():
            weight_copy(nth_straight(i + 3)).start()

        @pl.when(i + 1 < straight)
        def _():
            multiply(nth_straight(i + 1), False)

        @pl.when((i - 1 >= first_crossed) & (i - 1 < chunks - 1))
        def _():
            second(i - 1, True)

        @pl.when((i - 1 < first_crossed) | (i - 1 == chunks - 1))
        def _():
            second(i - 1, False)

        for k in range(2, stages):
            lag = 2 * k - 1

            @pl.when((i >= lag) & (i < chunks + lag))
            def _():
                later(k, i - lag)

        @pl.when(i >= 2 * stages - 1)
        def _():
            finish(i - (2 * stages - 1))

    @pl.loop(0, chunks)
    def _(c):
        for k in range(stages):
            exchange(k, c).wait_send()


def solution(mesh):
    wide = mesh.shape["wide"]
    stages = wide.bit_length() - 1

    def body(gate_pre, up_pre, down_weight):
        rows, depth = gate_pre.shape
        columns = down_weight.shape[1]
        mine = wide // 2
        block, tokens, chunks = rows // mine, 2 * rows, columns // TILE
        held = [(2, tokens // 4), *((tokens >> (k + 1),) for k in range(1, stages))]
        parts = [pltpu.VMEM((chunks, *rows_held, TILE), jnp.bfloat16) for rows_held in held]
        return pl.pallas_call(
            functools.partial(kernel, stages, block),
            out_shape=jax.ShapeDtypeStruct((block, columns), jnp.bfloat16),
            in_specs=[pl.BlockSpec(memory_space=pl.ANY)] * 3,
            out_specs=pl.BlockSpec(memory_space=pltpu.VMEM),
            scratch_shapes=[
                pltpu.VMEM((rows, depth), jnp.bfloat16),
                pltpu.VMEM((rows, depth), jnp.bfloat16),
                pltpu.VMEM((mine, 2, block, depth), jnp.bfloat16),
                pltpu.VMEM((chunks, depth, TILE), jnp.bfloat16),
                pltpu.VMEM((chunks, 2, 2, tokens // 4, TILE), jnp.float32),
                *parts,
                *parts,
                pltpu.SemaphoreType.DMA((2, mine)),
                pltpu.SemaphoreType.DMA((chunks,)),
                pltpu.SemaphoreType.DMA((mine,)),
                pltpu.SemaphoreType.DMA((mine,)),
                pltpu.SemaphoreType.DMA((stages, chunks)),
                pltpu.SemaphoreType.DMA((stages, chunks)),
            ],
            cost_estimate=pl.CostEstimate(
                flops=2 * tokens * depth * columns, bytes_accessed=2 * depth * columns, transcendentals=rows * depth
            ),
            compiler_params=pltpu.CompilerParams(
                collective_id=0, has_side_effects=True, vmem_limit_bytes=60 * 2**20
            ),
        )(gate_pre, up_pre, down_weight)

    return jax.shard_map(
        body,
        mesh=mesh,
        in_specs=(
            P(("groups", "narrow"), "wide"),
            P(("groups", "narrow"), "wide"),
            P("wide", "narrow"),
        ),
        out_specs=P(("groups", "wide"), "narrow"),
        check_vma=False,
    )
```

```python
import functools

import jax
import jax.numpy as jnp
from jax import lax
from jax.experimental import pallas as pl
from jax.experimental.pallas import tpu as pltpu
from jax.sharding import PartitionSpec as P

MESH = pl.DeviceIdType.MESH
TILE = 512
CROSSED = 2


def reverse(value, bits):
    return sum(((value >> i) & 1) << (bits - 1 - i) for i in range(bits))


def kernel(stages, block, gate_hbm, up_hbm, weight_hbm, out_ref, gate, up, hidden, weight, acc, *rest):
    sends, recvs = rest[:stages], rest[stages : 2 * stages]
    in_sem, weight_sem, gather_send, gather_recv, send_sem, recv_sem = rest[2 * stages :]
    chunks, depth, tile = weight.shape
    mine = hidden.shape[0]
    tokens = 2 * mine * block
    wide, core = lax.axis_index("wide"), lax.axis_index("narrow")
    bits = [(wide // 2**k) % 2 for k in range(stages)]
    partner = [wide + (1 - 2 * bits[k]) * 2**k for k in range(stages)]

    def fetch(j):
        rows = pl.ds(j * block, block)
        return (
            pltpu.make_async_copy(gate_hbm.at[rows], gate.at[rows], in_sem.at[0, j]),
            pltpu.make_async_copy(up_hbm.at[rows], up.at[rows], in_sem.at[1, j]),
        )

    def weight_copy(c):
        return pltpu.make_async_copy(
            weight_hbm.at[:, pl.ds(pl.multiple_of(c * tile, tile), tile)], weight.at[c], weight_sem.at[c]
        )

    def gather(j):
        place = hidden.at[reverse(j, stages - 1), core]
        return pltpu.make_async_remote_copy(
            src_ref=place,
            dst_ref=place,
            send_sem=gather_send.at[j],
            recv_sem=gather_recv.at[j],
            device_id={"narrow": 1 - core},
            device_id_type=MESH,
        )

    def exchange(k, c, crossed=False):
        to = partner[1 - k] if crossed and k < 2 else partner[k]
        return pltpu.make_async_remote_copy(
            src_ref=sends[k].at[c],
            dst_ref=recvs[k].at[c],
            send_sem=send_sem.at[k, c],
            recv_sem=recv_sem.at[k, c],
            device_id={"wide": to},
            device_id_type=MESH,
        )

    first_crossed = chunks - CROSSED - 1
    straight = chunks - CROSSED

    def nth_straight(i):
        return i + (i // first_crossed) * CROSSED

    for j in range(mine):
        for copy in fetch(j):
            copy.start()
    for c in (0, 1, *range(first_crossed, chunks - 1)):
        weight_copy(c).start()

    barrier = pltpu.get_barrier_semaphore()
    pl.semaphore_signal(barrier, inc=1, device_id={"narrow": 1 - core}, device_id_type=MESH)
    for k in range(stages):
        pl.semaphore_signal(barrier, inc=1, device_id={"wide": partner[k]}, device_id_type=MESH)
    pl.semaphore_wait(barrier, stages + 1)

    for j in range(mine):
        for copy in fetch(j):
            copy.wait()
        rows = pl.ds(j * block, block)
        value = jax.nn.silu(gate[rows].astype(jnp.float32)) * up[rows].astype(jnp.float32)
        hidden[reverse(j, stages - 1), core] = value.astype(jnp.bfloat16)
        gather(j).start()
    for i in range(2, straight):
        weight_copy(nth_straight(i)).start()
    for j in range(mine):
        gather(j).wait()

    b0, b1 = bits[:2]
    quarter = tokens // 4
    start = [None, None, 0]
    for k in range(2, stages):
        start.append(start[k] + bits[k] * (tokens >> (k + 1)))

    def multiply(c, crossed):
        weight_copy(c).wait()
        product = jnp.dot(hidden[...].reshape(tokens, depth), weight[c], preferred_element_type=jnp.float32)
        acc[c] = product.reshape(2, 2, quarter, tile)
        leaving = acc[c, :, 1 - b1] if crossed else acc[c, 1 - b0]
        sends[0][c] = leaving.astype(jnp.bfloat16)
        exchange(0, c, crossed).start()

    def second(c, crossed):
        exchange(0, c, crossed).wait_recv()
        o0, o1, other, own = (1 - b0, b1, 1 - b0, b0) if crossed else (b0, 1 - b1, 1 - b1, b1)
        sends[1][c] = (acc[c, o0, o1] + recvs[0][c, other].astype(jnp.float32)).astype(jnp.bfloat16)
        exchange(1, c, crossed).start()
        acc[c, b0, b1] += recvs[0][c, own].astype(jnp.float32)

    def later(k, c):
        exchange(k - 1, c).wait_recv()
        half = tokens >> (k + 1)
        other, own = (pl.multiple_of(bit * half, half) for bit in (1 - bits[k], bits[k]))
        sends[k][c] = (
            acc[c, b0, b1, pl.ds(pl.multiple_of(start[k] + other, half), half)]
            + recvs[k - 1][c, pl.ds(other, half)].astype(jnp.float32)
        ).astype(jnp.bfloat16)
        exchange(k, c).start()
        acc[c, b0, b1, pl.ds(pl.multiple_of(start[k] + own, half), half)] += recvs[k - 1][
            c, pl.ds(own, half)
        ].astype(jnp.float32)

    def finish(c):
        exchange(stages - 1, c).wait_recv()
        total = acc[c, b0, b1, pl.ds(pl.multiple_of(start[stages], block), block)]
        total += recvs[stages - 1][c].astype(jnp.float32)
        out_ref[:, pl.ds(pl.multiple_of(c * tile, tile), tile)] = total.astype(jnp.bfloat16)

    @pl.loop(0, 2)
    def _(c):
        multiply(c, False)

    @pl.loop(first_crossed, chunks - 1)
    def _(c):
        multiply(c, True)

    @pl.loop(1, chunks + 2 * stages - 1)
    def _(i):
        @pl.when(i + 1 < straight)
        def _():
            multiply(nth_straight(i + 1), False)

        @pl.when((i - 1 >= first_crossed) & (i - 1 < chunks - 1))
        def _():
            second(i - 1, True)

        @pl.when((i - 1 < first_crossed) | (i - 1 == chunks - 1))
        def _():
            second(i - 1, False)

        for k in range(2, stages):
            lag = 2 * k - 1

            @pl.when((i >= lag) & (i < chunks + lag))
            def _():
                later(k, i - lag)

        @pl.when(i >= 2 * stages - 1)
        def _():
            finish(i - (2 * stages - 1))

    @pl.loop(0, chunks)
    def _(c):
        for k in range(stages):
            exchange(k, c).wait_send()


def solution(mesh):
    wide = mesh.shape["wide"]
    stages = wide.bit_length() - 1

    def body(gate_pre, up_pre, down_weight):
        rows, depth = gate_pre.shape
        columns = down_weight.shape[1]
        mine = wide // 2
        block, tokens, chunks = rows // mine, 2 * rows, columns // TILE
        held = [(2, tokens // 4), *((tokens >> (k + 1),) for k in range(1, stages))]
        parts = [pltpu.VMEM((chunks, *rows_held, TILE), jnp.bfloat16) for rows_held in held]
        return pl.pallas_call(
            functools.partial(kernel, stages, block),
            out_shape=jax.ShapeDtypeStruct((block, columns), jnp.bfloat16),
            in_specs=[pl.BlockSpec(memory_space=pl.ANY)] * 3,
            out_specs=pl.BlockSpec(memory_space=pltpu.VMEM),
            scratch_shapes=[
                pltpu.VMEM((rows, depth), jnp.bfloat16),
                pltpu.VMEM((rows, depth), jnp.bfloat16),
                pltpu.VMEM((mine, 2, block, depth), jnp.bfloat16),
                pltpu.VMEM((chunks, depth, TILE), jnp.bfloat16),
                pltpu.VMEM((chunks, 2, 2, tokens // 4, TILE), jnp.float32),
                *parts,
                *parts,
                pltpu.SemaphoreType.DMA((2, mine)),
                pltpu.SemaphoreType.DMA((chunks,)),
                pltpu.SemaphoreType.DMA((mine,)),
                pltpu.SemaphoreType.DMA((mine,)),
                pltpu.SemaphoreType.DMA((stages, chunks)),
                pltpu.SemaphoreType.DMA((stages, chunks)),
            ],
            cost_estimate=pl.CostEstimate(
                flops=2 * tokens * depth * columns, bytes_accessed=2 * depth * columns, transcendentals=rows * depth
            ),
            compiler_params=pltpu.CompilerParams(
                collective_id=0, has_side_effects=True, vmem_limit_bytes=60 * 2**20
            ),
        )(gate_pre, up_pre, down_weight)

    return jax.shard_map(
        body,
        mesh=mesh,
        in_specs=(
            P(("groups", "narrow"), "wide"),
            P(("groups", "narrow"), "wide"),
            P("wide", "narrow"),
        ),
        out_specs=P(("groups", "wide"), "narrow"),
        check_vma=False,
    )
```
